256 devices in a mesh: row: 32 (over x, z_hi, core), col: 8 (over z_lo, y).
Axes of the slice: x: 4, y: 4, z: 8 (z_hi: 4, z_lo: 2; z = z_hi * 2 + z_lo), core: 2. Of those that a mesh axis runs over, the one named last changes fastest.
Arguments:
- grad_out: float32 [131072, 128], P(('col', 'row')), may hold values from -6 to 6
- features: float32 [131072, 128], P(('row', 'col')), may hold values from -0.015625 to 0.015625
- weight: float32 [128, 128], replicated, may hold values from -0.5 to 0.5
- adj_values: float32 [8, 1024, 3, 128, 128], P('col', 'row'), may hold values from -0.15625 to 0.15625
- row_block: int32 [8, 1024, 3], P('col', 'row'), may hold values from 0 to 3
- col_block: int32 [8, 1024, 3], P('col', 'row'), may hold values from 0 to 31
- counts: int32 [8, 1024], P('col', 'row'), may hold values from 0 to 3, as said below
Outputs:
- input_grad: float32 [131072, 128], P(('row', 'col'))
- weight_grad: float32 [128, 128], replicated
The draws below stay inside these ranges and needn't reach their ends.
Inputs may be any that keep to these rules, and one draw needn't show every extreme that they name: counts[c, j] is the number of leading slots of grid cell (c, j) that hold blocks of A; later slots hold values that are not part of A.
All inputs are finite; a program needn't handle non-finite values.
Results may differ from the reference program's by a relative error of at most 0.0003.
Values sent between devices are 32-bit elements; how exact they have to be, the bound alone decides.
A program may use at most 64 MiB of HBM per device.

```python
import jax
import jax.numpy as jnp
from jax import lax

WIDTH = 128
BLOCK = 128
SLOTS = 3
NODE_DEV = 512
ROW_BLOCKS = 4
COL_BLOCKS = 32
NODES = 131072
N_ROW = 32
N_COL = 8


def draw_counts(key, part):
    key = jax.random.fold_in(key, 7)
    first_key, second_key = jax.random.split(key)
    levels = jax.random.randint(first_key, (N_COL, N_ROW * N_ROW), 0, SLOTS + 1, dtype=jnp.int32)
    chosen = jax.random.randint(second_key, (N_COL, 1), 0, N_ROW * N_ROW, dtype=jnp.int32)
    section_ids = jnp.arange(N_ROW * N_ROW, dtype=jnp.int32)[None, :]
    return jnp.where(section_ids == chosen, SLOTS, levels).astype(jnp.int32)


def place_ends(array, own_key, smallest, high):
    extent = array.shape
    spot = [jax.random.randint(jax.random.fold_in(own_key, axis), (), 0, extent[axis]) for axis in range(len(extent))]
    array = array.at[tuple(spot)].set(smallest)
    longest = extent.index(max(extent))
    spot[longest] = (spot[longest] + 1) % extent[longest]
    return array.at[tuple(spot)].set(high)


def block_scale(own_key, dims, shards, smallest, high):
    loudness = 1.0
    for position, shards_of in shards:
        draws = jax.random.uniform(jax.random.fold_in(jax.random.fold_in(own_key, 6), position), (shards_of,), jnp.float32, smallest / len(shards), high / len(shards))
        loudness = loudness * jnp.repeat(jnp.exp(draws), dims[position] // shards_of).reshape((-1,) + (1,) * (len(dims) - 1 - position))
    return loudness


def gaussian(key, dims, deviation, limit, cuts=(), held_as=jnp.bfloat16):
    gain = block_scale(key, dims, cuts, -0.22, 0.18) if cuts else 1.0
    array = jax.random.normal(key, dims, jnp.float32) * deviation * gain
    return jnp.minimum(jnp.maximum(array, -limit), limit).astype(held_as)


def setup_inputs(seed: int = 0) -> dict:
    splits = jax.random.split(jax.random.key(seed), 8)
    return {
        "grad_out": gaussian(splits[0], (NODES, WIDTH), 1.0, 6.0, ((0, 256),), jnp.float32),
        "features": gaussian(splits[1], (NODES, WIDTH), NODES ** -0.5, 0.015625, ((0, 256),), jnp.float32),
        "weight": gaussian(splits[2], (WIDTH, WIDTH), WIDTH ** -0.5, 0.5, (), jnp.float32),
        "adj_values": gaussian(splits[3], (N_COL, N_ROW * N_ROW, SLOTS, BLOCK, BLOCK), (N_ROW * SLOTS * BLOCK * BLOCK // (2 * NODE_DEV)) ** -0.5, 0.15625, ((0, 8), (1, 32)), jnp.float32),
        "row_block": place_ends(jax.random.randint(splits[4], (N_COL, N_ROW * N_ROW, SLOTS), 0, ROW_BLOCKS), jax.random.fold_in(splits[4], 1), 0, ROW_BLOCKS - 1).astype(jnp.int32),
        "col_block": place_ends(jax.random.randint(splits[5], (N_COL, N_ROW * N_ROW, SLOTS), 0, COL_BLOCKS), jax.random.fold_in(splits[5], 1), 0, COL_BLOCKS - 1).astype(jnp.int32),
        "counts": draw_counts(jax.random.fold_in(splits[7], 71), 0),
    }


def reference(grad_out, features, weight, adj_values, row_block, col_block, counts):
    col_blocks = N_COL * NODE_DEV // BLOCK
    grad_blocks = grad_out.reshape(N_COL * N_ROW * ROW_BLOCKS, BLOCK, WIDTH)
    values = adj_values.reshape(N_COL, N_ROW, N_ROW, SLOTS, BLOCK, BLOCK)
    slot_rows = row_block.reshape(N_COL, N_ROW, N_ROW, SLOTS)
    slot_cols = col_block.reshape(N_COL, N_ROW, N_ROW, SLOTS)
    live_counts = counts.reshape(N_COL, N_ROW, N_ROW)
    base_rows = (jnp.arange(N_COL, dtype=jnp.int32)[:, None, None] * (N_ROW * ROW_BLOCKS)
                 + jnp.arange(N_ROW, dtype=jnp.int32)[None, :, None] * ROW_BLOCKS)
    slot_iota = jnp.arange(SLOTS, dtype=jnp.int32)
    col_iota = jnp.arange(col_blocks, dtype=jnp.int32)

    def column_part(part_index):
        part_values = values[:, part_index]
        flat_rows = (base_rows + slot_rows[:, part_index]).astype(jnp.int32)
        picked = grad_blocks[flat_rows]
        products = jnp.einsum('cksab,cksaf->cksbf', part_values, picked,
                              precision=lax.Precision.HIGHEST)
        live_slot = (slot_iota < live_counts[:, part_index][..., None]).astype(jnp.float32)
        onehot = (slot_cols[:, part_index][..., None] == col_iota).astype(jnp.float32) * live_slot[..., None]
        summed = jnp.einsum('cksm,cksbf->mbf', onehot, products,
                            precision=lax.Precision.HIGHEST)
        return summed.reshape(col_blocks * BLOCK, WIDTH)

    column_sums = lax.map(column_part, jnp.arange(N_ROW, dtype=jnp.int32)).reshape(NODES, WIDTH)
    input_grad = jnp.dot(column_sums, weight.T, precision=lax.Precision.HIGHEST,
                         preferred_element_type=jnp.float32)
    weight_grad = jnp.dot(features.T, column_sums, precision=lax.Precision.HIGHEST,
                          preferred_element_type=jnp.float32)
    return input_grad, weight_grad
```

```python
import functools

import jax
import jax.numpy as jnp
from jax import lax
from jax.experimental import pallas as pl
from jax.experimental.pallas import tpu as pltpu
from jax.sharding import PartitionSpec as P

WIDTH = 128
BLOCK = 128
SLOTS = 3
SECTIONS = 32
CELLS = SECTIONS * SLOTS
COL_BLOCKS = 32
CHUNKS = (32, 32, 32, 32)
BATCHES = ((0, 1, 2), (3,))
STAGES = {
    "T0": 0.0, "T1": 0.35, "T2": 0.75, "T3": 1.8, "T4": 2.4, "T5": 2.8,
    "C0": 2.81, "C1": 2.9, "C2": 3.1, "C3": 3.3,
    "R0": 3.32, "R1": 3.6, "R2": 3.9, "R3": 4.2,
}
MESH = pl.DeviceIdType.MESH
HIGHEST = lax.Precision.HIGHEST


def split(v):
    high = v.astype(jnp.bfloat16)
    return high, (v - high.astype(jnp.float32)).astype(jnp.bfloat16)


def starts():
    total, at = 0, []
    for f in CHUNKS:
        at.append(total)
        total += f
    return at


def kernel(
    meta, grad_hbm, feats_hbm, weight_hbm, adj_hbm, ig_out, wg_out,
    adj, halves, grad, feats, weight, run, csum, wgt, local_sem, send_sem, recv_sem, *bufs,
):
    n = len(CHUNKS)
    per = 8
    chunk_bufs = [bufs[per * j : per * (j + 1)] for j in range(n)]
    sum_bufs = [bufs[per * n + 3 * b : per * n + 3 * b + 3] for b in range(len(BATCHES))]
    at = starts()

    row, col = lax.axis_index("row"), lax.axis_index("col")
    x, zh, h = row // 8, (row // 2) % 4, row % 2
    zl, y = col // 4, col % 4
    corner = x * 2 + h

    def place(x_, zh_, h_):
        return {"row": x_ * 8 + zh_ * 2 + h_, "col": col}

    def place_col(zl_, y_):
        return {"row": row, "col": zl_ * 4 + y_}

    xp, xm, xo = (x + 1) % 4, (x + 3) % 4, (x + 2) % 4
    zp, zm, zo = (zh + 1) % 4, (zh + 3) % 4, (zh + 2) % 4
    yp, ym, yo = (y + 1) % 4, (y + 3) % 4, (y + 2) % 4
    sib = place(x, zh, 1 - h)
    to_xp, to_xm = place(xp, zh, h), place(xm, zh, h)
    to_zp, to_zm = place(x, zp, h), place(x, zm, h)
    to_yp, to_ym = place_col(zl, yp), place_col(zl, ym)
    to_zl = place_col(1 - zl, y)
    col_peers = [{"row": row, "col": (col + d) % 8} for d in range(1, 8)]
    corner_peers = []
    for d in range(1, 8):
        o = (corner + d) % 8
        corner_peers.append(place(o // 2, zh, o % 2))
    zh_peers = [place(x, (zh + d) % 4, h) for d in range(1, 4)]

    def load(k, src, dst):
        c = pltpu.make_async_copy(src, dst, local_sem.at[k])
        c.start()
        return c

    grad_load = load(0, grad_hbm, grad)
    adj_load = load(1, adj_hbm, adj)
    feats_load = load(2, feats_hbm, feats)
    weight_load = load(3, weight_hbm, weight)

    barrier = pltpu.get_barrier_semaphore()
    for peer in col_peers + corner_peers + zh_peers:
        pl.semaphore_signal(barrier, inc=1, device_id=peer, device_id_type=MESH)

    grad_load.wait()
    hx = h * 4 + x
    for rb in range(4):
        turned = grad[rb * BLOCK : (rb + 1) * BLOCK, :].T
        for j in range(n):
            chunk_bufs[j][0][hx, zh, rb] = turned[at[j] : at[j] + CHUNKS[j], :]

    pl.semaphore_wait(barrier, 17)

    sends = []

    def push(src, dst, peer):
        k = len(sends)
        c = pltpu.make_async_remote_copy(
            src_ref=src, dst_ref=dst, send_sem=send_sem.at[k], recv_sem=recv_sem.at[k],
            device_id=peer, device_id_type=MESH,
        )
        c.start()
        sends.append(c)
        return c

    pending = {}

    def move(ref, peer):
        return push(ref, ref, peer)

    def take(*key):
        for c in pending.pop(key):
            c.wait_recv()

    A, B = pl.ds(0, 3), pl.ds(3, 1)

    def stage_T0(j):
        g = chunk_bufs[j][0]
        pending["T0", j] = [
            move(g.at[hx, zh, A], to_zp), move(g.at[hx, zh, A], to_zm),
            move(g.at[hx, zh, B], to_xp), move(g.at[hx, zh, B], to_xm),
        ]

    def lows(j):
        half = CHUNKS[j] // 2
        return pl.ds(0, half), pl.ds(half, half)

    def stage_T1(j):
        g = chunk_bufs[j][0]
        lo, hi = lows(j)
        take("T0", j)
        pending["T1", j] = [
            move(g.at[hx, zm, A, lo], to_zp), move(g.at[hx, zp, A, hi], to_zm),
            move(g.at[h * 4 + xm, zh, B, lo], to_xp), move(g.at[h * 4 + xp, zh, B, hi], to_xm),
        ]

    ours = pl.ds(h * 4, 4)

    def stage_T2(j):
        g = chunk_bufs[j][0]
        take("T1", j)
        pending["T2", j] = [
            move(g.at[hx, :, A], to_xp), move(g.at[hx, :, A], to_xm),
            move(g.at[ours, zh, B], to_zp), move(g.at[ours, zh, B], to_zm),
        ]
        pending["S", j] = [move(g.at[hx, :, A], sib), move(g.at[ours, zh, B], sib)]

    def stage_T3(j):
        g = chunk_bufs[j][0]
        lo, hi = lows(j)
        take("T2", j)
        pending["T3", j] = [
            move(g.at[h * 4 + xm, :, A, lo], to_xp), move(g.at[h * 4 + xp, :, A, hi], to_xm),
            move(g.at[ours, zm, B, lo], to_zp), move(g.at[ours, zp, B, hi], to_zm),
        ]
        pending["S", j] += [
            move(g.at[h * 4 + xm, :, A], sib), move(g.at[h * 4 + xp, :, A], sib),
            move(g.at[ours, zm, B], sib), move(g.at[ours, zp, B], sib),
        ]

    def stage_T4(j):
        g = chunk_bufs[j][0]
        take("T3", j)
        pending["S", j] += [move(g.at[h * 4 + xo, :, A], sib), move(g.at[ours, zo, B], sib)]

    def stage_T5(j):
        take("S", j)

    def stage_C(j, part):
        g, part_sums = chunk_bufs[j][0], chunk_bufs[j][1]
        f = CHUNKS[j]
        size = CELLS // 4
        first = part * size

        def step(p, acc):
            block = halves[meta[0, p]]
            picked = g[meta[1, p], meta[2, p], meta[3, p]]
            high, low = split(picked)
            both = jnp.concatenate([high, low], axis=0)
            r = jnp.dot(both, block, preferred_element_type=jnp.float32)
            product = r[:f, :BLOCK] + (r[f:, :BLOCK] + r[:f, BLOCK:])
            acc = product + jnp.where(meta[4, p] > 0, acc, 0.0)
            run[p, :f] = acc
            return acc

        init = jnp.zeros((f, BLOCK), jnp.float32) if part == 0 else run[first - 1, :f]
        lax.fori_loop(first, first + size, step, init, unroll=4)
        if part == 3:
            def collect(m, carry):
                v = run[meta[5, m], :f]
                part_sums[m // 16, (m // 4) % 4, m % 4] = jnp.where(meta[6, m] > 0, v, 0.0)
                return carry

            lax.fori_loop(0, COL_BLOCKS, collect, 0, unroll=4)

    def stage_R0(j):
        p, r1p, r1m = chunk_bufs[j][1:4]
        pending["R0", j] = [
            push(p.at[:, yo, pl.ds(0, 2)], r1p, to_yp),
            push(p.at[:, yo, pl.ds(2, 2)], r1m, to_ym),
        ]

    def stage_R1(j):
        p, r1p, r1m, r2p, r2m = chunk_bufs[j][1:6]
        take("R0", j)
        for z in range(2):
            p[z, yp, 0:2] = p[z, yp, 0:2] + r1p[z]
            p[z, ym, 2:4] = p[z, ym, 2:4] + r1m[z]
        pending["R1", j] = [push(p.at[:, yp], r2p, to_yp), push(p.at[:, ym], r2m, to_ym)]

    def stage_R2(j):
        p, r1p, r1m, r2p, r2m, s, r3 = chunk_bufs[j][1:8]
        take("R1", j)
        for z in range(2):
            s[z] = p[z, y] + (r2p[z] + r2m[z])
        pending["R2", j] = [push(s.at[1 - zl], r3, to_zl)]

    def stage_R3(j):
        s, r3 = chunk_bufs[j][6:8]
        take("R2", j)
        f = CHUNKS[j]
        total = jnp.zeros((f, WIDTH), jnp.float32)
        for b in range(4):
            v = s[zl, b] + r3[b]
            csum[b, at[j] : at[j] + f, :] = v
            total += jnp.dot(
                v, feats[b * BLOCK : (b + 1) * BLOCK, :], precision=HIGHEST,
                preferred_element_type=jnp.float32,
            )
        wgt[at[j] : at[j] + f, :] = total

    def window(b):
        first = at[BATCHES[b][0]]
        return pl.ds(first, sum(CHUNKS[j] for j in BATCHES[b]))

    def fold(buf, count):
        total = buf[0]
        for i in range(1, count):
            total += buf[i]
        return total

    def stage_W0(b):
        buf = sum_bufs[b][0]
        buf[col] = wgt[window(b), :]
        pending["W0", b] = [push(buf.at[col], buf.at[col], peer) for peer in col_peers]

    def stage_W1(b):
        take("W0", b)
        buf = sum_bufs[b][1]
        buf[corner] = fold(sum_bufs[b][0], 8)
        pending["W1", b] = [push(buf.at[corner], buf.at[corner], peer) for peer in corner_peers]

    def stage_W2(b):
        take("W1", b)
        buf = sum_bufs[b][2]
        buf[zh] = fold(sum_bufs[b][1], 8)
        pending["W2", b] = [push(buf.at[zh], buf.at[zh], peer) for peer in zh_peers]

    def stage_W3(b):
        take("W2", b)
        wgt[window(b), :] = fold(sum_bufs[b][2], 4)

    unit = CHUNKS[0]
    plan = []
    for j in range(n):
        begin = at[j] / unit
        for name, offset in STAGES.items():
            plan.append((begin + offset, len(plan), name, j))
    for b, batch in enumerate(BATCHES):
        begin = at[batch[-1]] / unit + STAGES["R3"]
        for i in range(4):
            plan.append((begin + 0.01 + 0.3 * i, len(plan), "W" + str(i), b))
    plan.sort()

    split_parts = 4
    done_split = 0

    def split_part(i):
        if i == 0:
            adj_load.wait()
        size = CELLS // split_parts

        def body(s, carry):
            high, low = split(adj[s])
            halves[s, :, :BLOCK] = high
            halves[s, :, BLOCK:] = low
            return carry

        lax.fori_loop(i * size, (i + 1) * size, body, 0, unroll=2)

    for _, _, name, j in plan:
        if name == "R3" and j == 0:
            feats_load.wait()
            weight_load.wait()
        if name == "W1" and j == len(BATCHES) - 1:
            turned_weight = weight[...].T
            for b in range(4):
                ig_out[b * BLOCK : (b + 1) * BLOCK, :] = jnp.dot(
                    csum[b].T, turned_weight, precision=HIGHEST, preferred_element_type=jnp.float32
                )
        if name[0] == "C":
            stage_C(j, int(name[1]))
        elif name[0] == "T":
            (stage_T0, stage_T1, stage_T2, stage_T3, stage_T4, stage_T5)[int(name[1])](j)
            if done_split < split_parts:
                split_part(done_split)
                done_split += 1
        elif name[0] == "R":
            (stage_R0, stage_R1, stage_R2, stage_R3)[int(name[1])](j)
        else:
            (stage_W0, stage_W1, stage_W2, stage_W3)[int(name[1])](j)

    wg_out[...] = wgt[...].T
    for c in sends:
        c.wait_send()


def scratch():
    f32 = jnp.float32
    out = [
        pltpu.VMEM((CELLS, BLOCK, BLOCK), f32),
        pltpu.VMEM((CELLS, BLOCK, 2 * BLOCK), jnp.bfloat16),
        pltpu.VMEM((512, WIDTH), f32),
        pltpu.VMEM((512, WIDTH), f32),
        pltpu.VMEM((WIDTH, WIDTH), f32),
        pltpu.VMEM((CELLS, max(CHUNKS), BLOCK), f32),
        pltpu.VMEM((4, WIDTH, BLOCK), f32),
        pltpu.VMEM((WIDTH, WIDTH), f32),
        pltpu.SemaphoreType.DMA((4,)),
    ]
    count = 29 * len(CHUNKS) + 17 * len(BATCHES)
    out += [pltpu.SemaphoreType.DMA((count,)), pltpu.SemaphoreType.DMA((count,))]
    for f in CHUNKS:
        for lead in ((8, 4, 4), (2, 4, 4), (2, 2), (2, 2), (2, 4), (2, 4), (2, 4), (4,)):
            out.append(pltpu.VMEM(lead + (f, BLOCK), f32))
    for batch in BATCHES:
        f = sum(CHUNKS[j] for j in batch)
        for lead in (8, 8, 4):
            out.append(pltpu.VMEM((lead, f, WIDTH), f32))
    return out


def prepare(row_block, col_block, counts):
    index = jnp.arange(CELLS, dtype=jnp.int32)
    k = index // SLOTS
    live = (jnp.arange(SLOTS, dtype=jnp.int32)[None, :] < counts[:, None]).reshape(CELLS)
    blocks = jnp.where(live, col_block.reshape(CELLS), COL_BLOCKS)
    keys = blocks * 128 + index
    rank = jnp.sum((keys[None, :] < keys[:, None]).astype(jnp.int32), axis=1)
    place = jnp.arange(128, dtype=jnp.int32)
    hit = rank[:, None] == place[None, :]
    fields = jnp.stack(
        [index, (k % 2) * 4 + k // 8, (k // 2) % 4, row_block.reshape(CELLS), blocks]
    )
    ordered = jnp.sum(jnp.where(hit[None], fields[:, :, None], 0), axis=1)
    same = jnp.concatenate(
        [jnp.zeros((1,), jnp.int32), (ordered[4, 1:] == ordered[4, :-1]).astype(jnp.int32)]
    )
    upto = jnp.sum((blocks[:, None] <= place[None, :]).astype(jnp.int32), axis=0)
    present = jnp.any(blocks[:, None] == place[None, :], axis=0).astype(jnp.int32)
    last = jnp.maximum(upto - 1, 0)
    return jnp.concatenate([ordered[:4], same[None], last[None], present[None]], axis=0)


def local(grad_out, features, weight, adj_values, row_block, col_block, counts):
    meta = prepare(row_block[0], col_block[0], counts[0])
    anyspace = pl.BlockSpec(memory_space=pl.ANY)
    return pl.pallas_call(
        kernel,
        out_shape=(
            jax.ShapeDtypeStruct((512, WIDTH), jnp.float32),
            jax.ShapeDtypeStruct((WIDTH, WIDTH), jnp.float32),
        ),
        in_specs=[pl.BlockSpec(memory_space=pltpu.SMEM)] + [anyspace] * 4,
        out_specs=(pl.BlockSpec(memory_space=pltpu.VMEM),) * 2,
        scratch_shapes=scratch(),
        compiler_params=pltpu.CompilerParams(
            collective_id=0, has_side_effects=True, vmem_limit_bytes=52 * 1024 * 1024
        ),
        cost_estimate=pl.CostEstimate(
            flops=1_200_000_000, bytes_accessed=7_000_000, transcendentals=0
        ),
    )(meta, grad_out, features, weight, adj_values.reshape(CELLS, BLOCK, BLOCK))


def solution(mesh):
    return jax.shard_map(
        local,
        mesh=mesh,
        in_specs=(
            P(("col", "row"), None),
            P(("row", "col"), None),
            P(),
            P("col", "row", None, None, None),
            P("col", "row", None),
            P("col", "row", None),
            P("col", "row"),
        ),
        out_specs=(P(("row", "col"), None), P()),
        check_vma=False,
    )
```

```python
import jax
import jax.numpy as jnp
from jax import lax
from jax.experimental import pallas as pl
from jax.experimental.pallas import tpu as pltpu
from jax.sharding import PartitionSpec as P

WIDTH = 128
BLOCK = 128
SLOTS = 3
SECTIONS = 32
CELLS = SECTIONS * SLOTS
GROUPS = ((0, 24), (24, 48), (72, 24))
PARTS = ((0, 0, 24), (1, 24, 24), (1, 48, 24), (2, 72, 24))
COL_BLOCKS = 32
NODE_DEV = 512
CHUNKS = (16, 32, 32, 32, 16)
ACROSS = (1, 1, 1, 0, 0)
STRAIGHT = (0, 0, 0, 0, 1)
EARLY = 4
ORDER = (
    ("U0", 0), ("U0", 1), ("U0", 2), ("U1", 0), ("U1", 1), ("U1", 2), ("U2", 0), ("C0", 0), ("U0", 3), ("U2", 1),
    ("C0", 1), ("U2", 2), ("U3", 0), ("C0", 2), ("U0", 4), ("C1", 0), ("C2", 0), ("U1", 3), ("U3", 1), ("U3", 2),
    ("U4", 0), ("C1", 1), ("C2", 1), ("U1", 4), ("C1", 2), ("C3", 0), ("R0", 0), ("U2", 3), ("U4", 1), ("C2", 2),
    ("U4", 2), ("C0", 3), ("C3", 1), ("U2", 4), ("R0", 1), ("C3", 2), ("R0", 2), ("C0", 4), ("U3", 3), ("R1", 0),
    ("U3", 4), ("C1", 3), ("C2", 3), ("U4", 3), ("C1", 4), ("R2", 0), ("U4", 4), ("C2", 4), ("C3", 3), ("R0", 3),
    ("C3", 4), ("R0", 4), ("R1", 1), ("R1", 2), ("R2", 1), ("R2", 2), ("R1", 3), ("R2", 4), ("W0", 0), ("R2", 3),
    ("V0", 0), ("O0", 0), ("W1", 0), ("V1", 0), ("W2", 0), ("V2", 0), ("V3", 0),
)
MESH = pl.DeviceIdType.MESH
HIGHEST = lax.Precision.HIGHEST


def starts():
    total, at = 0, []
    for f in CHUNKS:
        at.append(total)
        total += f
    return at


def split(v):
    high = v.astype(jnp.bfloat16).astype(jnp.float32)
    return high, v - high


def order_slots(rowb, colb, counts, x, zh, h, zl, y):
    lanes = lax.broadcasted_iota(jnp.int32, (1, BLOCK), 1)
    k, s = lanes & 31, lanes >> 5
    spare = jnp.zeros((1, SECTIONS), jnp.int32)

    def flat(ref):
        return jnp.concatenate([ref[0:1, :], ref[1:2, :], ref[2:3, :], spare], axis=1)

    rb, cb = flat(rowb), flat(colb)
    live = s < jnp.concatenate([counts[0:1, :]] * 4, axis=1)
    dx = ((k >> 3) - x + 4) & 3
    group = jnp.where(s == SLOTS, 3, jnp.where(dx == 0, 0, jnp.where(dx == 2, 2, 1)))
    key = ((group * 64 + jnp.where(live, cb, COL_BLOCKS)) * 128 + lanes) * 4 + rb
    across = jnp.broadcast_to(key, (BLOCK, BLOCK))
    down = across.T
    rank = jnp.sum((across < down).astype(jnp.int32), axis=1, keepdims=True)
    spot = lax.broadcasted_iota(jnp.int32, (BLOCK, BLOCK), 1)
    okey = jnp.sum(jnp.where(rank == spot, down, 0), axis=0, keepdims=True)
    oi = (okey >> 2) & 127
    ok, block = oi & 31, (okey >> 9) & 63
    odx, odz = ((ok >> 3) - x + 4) & 3, (((ok >> 1) & 3) - zh + 4) & 3
    before = pltpu.roll(block, 1, 1)
    first = (lanes == 0) | (lanes == GROUPS[1][0]) | (lanes == GROUPS[2][0])
    keep = jnp.where((block == before) & jnp.logical_not(first), 1, 0)
    zpos = jnp.where(odz == 0, 2, jnp.where(odz == 1, 0, jnp.where(odz == 2, 3, 1)))
    rows = [
        ok * SLOTS + (oi >> 5), jnp.where(odx == 3, 1, 0), (ok + h) & 1, zpos, okey & 3, keep,
    ]
    owner, column = down >> 15, (down >> 9) & 63
    wanted = (((spot >> 4) + zl) & 1) * 16 + (((spot >> 2) + y) & 3) * 4 + (spot & 3)
    for g, (begin, _) in enumerate(GROUPS):
        ours = owner == g
        upto = jnp.sum((ours & (column <= wanted)).astype(jnp.int32), axis=0, keepdims=True)
        here = jnp.sum((ours & (column == wanted)).astype(jnp.int32), axis=0, keepdims=True)
        rows.append(jnp.where(here > 0, begin + upto - 1, CELLS))
    return rows


def kernel(
    rowb, colb, counts, grad_hbm, feats_hbm, weight_hbm, adj_hbm, ig_out, wg_out,
    adj, halves, grad, feats, weight, csum, ig, wg, wgt, wgl, wgf, ordered, meta,
    tiles, crossed, late0, late1, local_sem, send_sem, recv_sem, *bufs,
):
    n = len(CHUNKS)
    at = starts()
    chunk_bufs = [bufs[8 * j : 8 * (j + 1)] for j in range(n)]

    row, col = lax.axis_index("row"), lax.axis_index("col")
    x, zh, h = row // 8, (row // 2) % 4, row % 2
    zl, y = col // 4, col % 4
    deck = zh * 4 + zl * 2 + h
    pillar = x * 4 + y

    def chip(dx, dz):
        return {"row": ((x + dx) % 4) * 8 + ((zh + dz) % 4) * 2 + h, "col": col}

    def on_pillar(d):
        o = (pillar + d) % 16
        return {"row": (o // 4) * 8 + zh * 2 + h, "col": zl * 4 + o % 4}

    def on_deck(d):
        o = (deck + d) % 16
        return {"row": x * 8 + (o // 4) * 2 + o % 2, "col": ((o // 2) % 2) * 4 + y}

    def in_col(dzl, dy):
        return {"row": row, "col": ((zl + dzl) % 2) * 4 + (y + dy) % 4}

    sib = {"row": x * 8 + zh * 2 + 1 - h, "col": col}
    xp, xm, zp, zm = chip(1, 0), chip(3, 0), chip(0, 1), chip(0, 3)
    pillar_peers = [on_pillar(d) for d in range(1, 16)]
    deck_peers = [on_deck(d) for d in range(1, 16)]
    col_steps = [(a, b) for a in range(2) for b in range(4) if (a, b) != (0, 0)]
    col_peers = {step: in_col(*step) for step in col_steps}

    def load(k, src, dst):
        c = pltpu.make_async_copy(src, dst, local_sem.at[k])
        c.start()
        return c

    grad_load = load(0, grad_hbm, grad)
    adj_load = load(1, adj_hbm, adj)
    feats_load = load(2, feats_hbm, feats)
    weight_load = load(3, weight_hbm, weight)

    barrier = pltpu.get_barrier_semaphore()
    greeted = pillar_peers + deck_peers + [col_peers[1, d] for d in range(1, 4)]
    for peer in greeted:
        pl.semaphore_signal(barrier, inc=1, device_id=peer, device_id_type=MESH)

    grad_load.wait()
    for rb in range(4):
        turned = grad[rb * BLOCK : (rb + 1) * BLOCK, :].T
        for j in range(n):
            chunk_bufs[j][0][0, 0, 2, rb] = turned[at[j] : at[j] + CHUNKS[j], :]
    pl.semaphore_wait(barrier, len(greeted))

    sends = []
    pending = {}

    def push(key, src, dst, peer):
        k = len(sends)
        c = pltpu.make_async_remote_copy(
            src_ref=src, dst_ref=dst, send_sem=send_sem.at[k], recv_sem=recv_sem.at[k],
            device_id=peer, device_id_type=MESH,
        )
        c.start()
        sends.append(c)
        pending.setdefault(key, []).append(c)

    def take(*key):
        for c in pending.pop(key):
            c.wait_recv()

    def stage_U(j, d):
        near, mid, far = chunk_bufs[j][:3]
        f, cross = CHUNKS[j], ACROSS[j]
        down, over = pl.ds(0, 4 - cross), pl.ds(4 - cross, cross)
        every = pl.ds(0, 4)

        def half(blocks, i):
            if cross:
                return blocks, pl.ds(i * (f // 2), f // 2)
            return (pl.ds(2 * i, 2),)

        def go(key, src, dst, peer, *index):
            push((key, j), src.at[index], dst.at[index], peer)

        own, plus, minus, both, opposite = 2, 0, 1, pl.ds(0, 2), 3
        if d == 0:
            unit = near.at[0, 0, own]
            go("X0", unit, mid.at[1, 0, own], xp, every)
            go("X0", unit, mid.at[0, 0, own], xm, every)
            go("Z0", unit, near.at[0, 0, minus], zp, every)
            go("Z0", unit, near.at[0, 0, plus], zm, every)
        elif d == 1:
            take("X0", j)
            go("1", mid.at[1, 0, own], far.at[0, 0, own], xp, *half(every, 0))
            go("1", mid.at[0, 0, own], far.at[0, 0, own], xm, *half(every, 1))
            if cross:
                pair = mid.at[:, 0, own, over]
                push(("1", j), pair, mid.at[:, 0, minus, over], zp)
                push(("1", j), pair, mid.at[:, 0, plus, over], zm)
            take("Z0", j)
            go("1", near.at[0, 0, minus], near.at[0, 0, opposite], zp, *half(every, 0))
            go("1", near.at[0, 0, plus], near.at[0, 0, opposite], zm, *half(every, 1))
            pair = near.at[0, 0, both, down]
            push(("1", j), pair, mid.at[1, 0, both, down], xp)
            push(("1", j), pair, mid.at[0, 0, both, down], xm)
        elif d == 2:
            take("1", j)
            push(("2", j), near.at[0, 0, opposite, down], mid.at[1, 0, opposite, down], xp)
            push(("2", j), near.at[0, 0, opposite, down], mid.at[0, 0, opposite, down], xm)
            go("2", mid.at[1, 0], far.at[0, 0], xp, both, *half(down, 0))
            go("2", mid.at[0, 0], far.at[0, 0], xm, both, *half(down, 1))
            if cross:
                push(("2", j), far.at[0, 0, own, over], far.at[0, 0, minus, over], zp)
                push(("2", j), far.at[0, 0, own, over], far.at[0, 0, plus, over], zm)
                lo, hi = half(over, 0), half(over, 1)
                push(("2", j), mid.at[:, 0, minus, *lo], mid.at[:, 0, opposite, *lo], zp)
                push(("2", j), mid.at[:, 0, plus, *hi], mid.at[:, 0, opposite, *hi], zm)
            push(("S", j, 0), near.at[:, 0], near.at[:, 1], sib)
        elif d == 3:
            take("2", j)
            go("3", mid.at[1, 0, opposite], far.at[0, 0, opposite], xp, *half(down, 0))
            go("3", mid.at[0, 0, opposite], far.at[0, 0, opposite], xm, *half(down, 1))
            if cross:
                go("3", far.at[0, 0, minus], far.at[0, 0, opposite], zp, *half(over, 0))
                go("3", far.at[0, 0, plus], far.at[0, 0, opposite], zm, *half(over, 1))
            push(("S", j, 1), mid.at[:, 0], mid.at[:, 1], sib)
        else:
            take("3", j)
            push(("S", j, 2), far.at[:, 0], far.at[:, 1], sib)

    def stage_C(j, part):
        group, begin, size = PARTS[part]
        g, run, f = chunk_bufs[j][group], chunk_bufs[j][7], CHUNKS[j]
        if begin == GROUPS[group][0]:
            take("S", j, group)
            init = jnp.zeros((f, BLOCK), jnp.float32)
        else:
            init = run[begin - 1]

        def step(p, acc):
            block = halves[meta[0, p]]
            high, low = split(g[meta[1, p] if group == 1 else 0, meta[2, p], meta[3, p], meta[4, p]])
            both = jnp.concatenate([high, low], axis=0).astype(jnp.bfloat16)
            r = jnp.dot(both, block, preferred_element_type=jnp.float32)
            product = r[:f, :BLOCK] + (r[f:, :BLOCK] + r[:f, BLOCK:])
            acc = product + jnp.where(meta[5, p] > 0, acc, 0.0)
            run[p] = acc
            return acc

        lax.fori_loop(begin, begin + size, step, init, unroll=4)

    def collect(j):
        part_sums, run = chunk_bufs[j][3], chunk_bufs[j][7]
        run[CELLS] = jnp.zeros((CHUNKS[j], BLOCK), jnp.float32)

        def body(m, carry):
            v = [run[meta[6 + g, m]] for g in range(3)]
            part_sums[m // 16, (m // 4) % 4, m % 4] = (v[0] + v[1]) + v[2]
            return carry

        lax.fori_loop(0, COL_BLOCKS, body, 0, unroll=4)

    def stage_R0(j):
        collect(j)
        p, landing = chunk_bufs[j][3:5]
        if STRAIGHT[j]:
            for i, (a, b) in enumerate(col_steps):
                push(("R0", j), p.at[a, b], landing.at[i], col_peers[a, b])
        else:
            for d in range(1, 4):
                push(("R0", j), p.at[:, d], landing.at[d - 1], col_peers[0, d])

    def stage_R1(j):
        p, landing, s, second = chunk_bufs[j][3:7]
        take("R0", j)
        for z in range(2):
            s[z] = (p[z, 0] + landing[0, z]) + (landing[1, z] + landing[2, z])
        push(("R1", j), s.at[1], second, col_peers[1, 0])

    def stage_R2(j):
        p, landing, s, second = chunk_bufs[j][3:7]
        f = CHUNKS[j]
        take("R0" if STRAIGHT[j] else "R1", j)
        total = jnp.zeros((f, WIDTH), jnp.float32)
        for b in range(4):
            if STRAIGHT[j]:
                v = p[0, 0, b]
                for i in range(7):
                    v += landing[i, b]
            else:
                v = s[0, b] + second[b]
            csum[b, at[j] : at[j] + f, :] = v
            total += jnp.dot(
                v, feats[b * BLOCK : (b + 1) * BLOCK, :], precision=HIGHEST,
                preferred_element_type=jnp.float32,
            )
        if j < EARLY:
            wgt[at[j] : at[j] + f, :] = total
        else:
            wgl[at[j] - at[EARLY] : at[j] - at[EARLY] + f, :] = total

    def fold(buf):
        total = buf[0]
        for i in range(1, 16):
            total += buf[i]
        return total

    def tile(ref, i):
        return ref.at[pl.ds(pl.multiple_of(i * 8, 8), 8)]

    def stage_V(i):
        if i == 0:
            wgt[at[EARLY] :, :] = jnp.zeros((WIDTH - at[EARLY], WIDTH), jnp.float32)
            for d in range(1, 16):
                to = (pillar + d) % 16
                push(("V0",), tile(wgt, to), tiles.at[pillar], pillar_peers[d - 1])
            tiles[pillar] = wgt[pl.ds(pl.multiple_of(pillar * 8, 8), 8), :]
        elif i == 1:
            take("V0")
            crossed[deck] = fold(tiles)
            for d in range(1, 16):
                push(("V1",), crossed.at[deck], crossed.at[deck], deck_peers[d - 1])
        elif i == 2:
            take("V1")
            wgf[pl.ds(pl.multiple_of(pillar * 8, 8), 8), :] = fold(crossed)
            for d in range(1, 16):
                push(("V2",), tile(wgf, pillar), tile(wgf, pillar), pillar_peers[d - 1])
        else:
            take("V2")

    def stage_W(i):
        if i == 0:
            late0[pillar] = wgl[...]
            for d in range(1, 16):
                push(("W0",), late0.at[pillar], late0.at[pillar], pillar_peers[d - 1])
        elif i == 1:
            take("W0")
            late1[deck] = fold(late0)
            for d in range(1, 16):
                push(("W1",), late1.at[deck], late1.at[deck], deck_peers[d - 1])
        else:
            take("W1")

    parts, state = 8, {"done": 0, "sent": 0, "feats": False}

    def prepare():
        i = state["done"]
        state["done"] += 1
        if i == 0:
            ordered[...] = jnp.zeros((16, BLOCK), jnp.int32)
            for r, v in enumerate(order_slots(rowb, colb, counts, x, zh, h, zl, y)):
                ordered[r : r + 1, :] = v
            state["meta"] = load(4, ordered, meta)
            return
        if i == 1:
            adj_load.wait()
            state["meta"].wait()
        if i <= parts:
            size = CELLS // parts

            def body(s, carry):
                high, low = split(adj[s])
                halves[s, :, :BLOCK] = high.astype(jnp.bfloat16)
                halves[s, :, BLOCK:] = low.astype(jnp.bfloat16)
                return carry

            lax.fori_loop((i - 1) * size, i * size, body, 0, unroll=2)

    def drain(upto):
        while state["sent"] < upto:
            sends[state["sent"]].wait_send()
            state["sent"] += 1

    for name, j in ORDER:
        kind, i = name[0], int(name[1])
        if kind == "C":
            while state["done"] <= parts:
                prepare()
        if kind == "U":
            stage_U(j, i)
            prepare()
        elif kind == "C":
            stage_C(j, i)
        elif kind == "R":
            if name == "R2" and not state["feats"]:
                state["feats"] = True
                feats_load.wait()
            (stage_R0, stage_R1, stage_R2)[i](j)
        elif kind == "W":
            stage_W(i)
        elif kind == "V":
            stage_V(i)
            drain(len(sends) - 60)
        else:
            weight_load.wait()
            turned_weight = weight[...].T
            for b in range(4):
                ig[b * BLOCK : (b + 1) * BLOCK, :] = jnp.dot(
                    csum[b].T, turned_weight, precision=HIGHEST,
                    preferred_element_type=jnp.float32,
                )
            ig_store = load(0, ig, ig_out)

    wg[...] = jnp.concatenate([wgf[: at[EARLY], :], fold(late1)], axis=0).T
    wg_store = load(1, wg, wg_out)
    drain(len(sends))
    ig_store.wait()
    wg_store.wait()


def scratch():
    f32 = jnp.float32
    late = sum(CHUNKS[EARLY:])
    out = [
        pltpu.VMEM((CELLS, BLOCK, BLOCK), f32),
        pltpu.VMEM((CELLS, BLOCK, 2 * BLOCK), jnp.bfloat16),
        pltpu.VMEM((NODE_DEV, WIDTH), f32),
        pltpu.VMEM((NODE_DEV, WIDTH), f32),
        pltpu.VMEM((WIDTH, WIDTH), f32),
        pltpu.VMEM((4, WIDTH, BLOCK), f32),
        pltpu.VMEM((NODE_DEV, WIDTH), f32),
        pltpu.VMEM((WIDTH, WIDTH), f32),
        pltpu.VMEM((WIDTH, WIDTH), f32),
        pltpu.VMEM((late, WIDTH), f32),
        pltpu.VMEM((WIDTH, WIDTH), f32),
        pltpu.VMEM((16, BLOCK), jnp.int32),
        pltpu.SMEM((16, BLOCK), jnp.int32),
        pltpu.VMEM((16, 8, WIDTH), f32),
        pltpu.VMEM((16, 8, WIDTH), f32),
        pltpu.VMEM((16, late, WIDTH), f32),
        pltpu.VMEM((16, late, WIDTH), f32),
        pltpu.SemaphoreType.DMA((5,)),
    ]
    count = 34 * len(CHUNKS) + 80
    out += [pltpu.SemaphoreType.DMA((count,)), pltpu.SemaphoreType.DMA((count,))]
    for j, f in enumerate(CHUNKS):
        landing = (7, 4) if STRAIGHT[j] else (3, 2, 4)
        for lead in (
            (1, 2, 4, 4), (2, 2, 4, 4), (1, 2, 4, 4), (2, 4, 4), landing, (2, 4), (4,),
            (CELLS + 1,),
        ):
            out.append(pltpu.VMEM(lead + (f, BLOCK), f32))
    return out


def local(grad_out, features, weight, adj_values, row_block, col_block, counts):
    anyspace = pl.BlockSpec(memory_space=pl.ANY)
    vmem = pl.BlockSpec(memory_space=pltpu.VMEM)
    return pl.pallas_call(
        kernel,
        out_shape=(
            jax.ShapeDtypeStruct((NODE_DEV, WIDTH), jnp.float32),
            jax.ShapeDtypeStruct((WIDTH, WIDTH), jnp.float32),
        ),
        in_specs=[vmem] * 3 + [anyspace] * 4,
        out_specs=(anyspace, anyspace),
        scratch_shapes=scratch(),
        compiler_params=pltpu.CompilerParams(
            collective_id=0, has_side_effects=True, vmem_limit_bytes=60 * 1024 * 1024
        ),
        cost_estimate=pl.CostEstimate(
            flops=1_200_000_000, bytes_accessed=7_000_000, transcendentals=0
        ),
    )(
        row_block[0].T, col_block[0].T, counts, grad_out, features, weight,
        adj_values.reshape(CELLS, BLOCK, BLOCK),
    )


def solution(mesh):
    return jax.shard_map(
        local,
        mesh=mesh,
        in_specs=(
            P(("col", "row"), None),
            P(("row", "col"), None),
            P(),
            P("col", "row", None, None, None),
            P("col", "row", None),
            P("col", "row", None),
            P("col", "row"),
        ),
        out_specs=(P(("row", "col"), None), P()),
        check_vma=False,
    )
```

```python
import jax
import jax.numpy as jnp
from jax import lax
from jax.experimental import pallas as pl
from jax.experimental.pallas import tpu as pltpu
from jax.sharding import PartitionSpec as P

WIDTH = 128
BLOCK = 128
SLOTS = 3
SECTIONS = 32
CELLS = SECTIONS * SLOTS
GROUPS = ((0, 24), (24, 48), (72, 24))
PARTS = ((0, 0, 24), (1, 24, 24), (1, 48, 24), (2, 72, 24))
COL_BLOCKS = 32
NODE_DEV = 512
CHUNKS = (24, 40, 40, 24)
ACROSS = (0, 0, 1, 1)
ROUTES = ('y', 'y', 'y', 'z')
EARLY = 3
ORDER = (
    ("U0", 0), ("U0", 1), ("F0", 0), ("U1", 0), ("U1", 1), ("F1", 0), ("F2", 0), ("U0", 2), ("U2", 0), ("U0", 3),
    ("C0", 0), ("U2", 1), ("C0", 1), ("F3", 0), ("U3", 0), ("U1", 2), ("C1", 0), ("C2", 0), ("U1", 3), ("U3", 1),
    ("U4", 0), ("F4", 0), ("C1", 1), ("C3", 0), ("R0", 0), ("U2", 2), ("G0", 0), ("C2", 1), ("C0", 2), ("U2", 3),
    ("U4", 1), ("C0", 3), ("C3", 1), ("R0", 1), ("U3", 2), ("G0", 1), ("R1", 0), ("U3", 3), ("C1", 2), ("C2", 2),
    ("U4", 2), ("C1", 3), ("C2", 3), ("R2", 0), ("C3", 2), ("U4", 3), ("R0", 2), ("G0", 2), ("V0", 0), ("C3", 3),
    ("R0", 3), ("G0", 3), ("W0", 0), ("R1", 1), ("V1", 0), ("R1", 3), ("R1", 2), ("R2", 1), ("V2", 0), ("W1", 0),
    ("R2", 3), ("R2", 2), ("O0", 0), ("V3", 0), ("W2", 0),
)
MESH = pl.DeviceIdType.MESH
HIGHEST = lax.Precision.HIGHEST


def starts():
    total, at = 0, []
    for f in CHUNKS:
        at.append(total)
        total += f
    return at


def split(v):
    high = v.astype(jnp.bfloat16).astype(jnp.float32)
    return high, v - high


def order_slots(rowb, colb, counts, x, zh, h, zl, y):
    lanes = lax.broadcasted_iota(jnp.int32, (1, BLOCK), 1)
    k, s = lanes & 31, lanes >> 5
    spare = jnp.zeros((1, SECTIONS), jnp.int32)

    def flat(ref):
        return jnp.concatenate([ref[0], ref[1], ref[2], spare], axis=1)

    rb, cb = flat(rowb), flat(colb)
    live = s < jnp.concatenate([counts[0:1, :]] * 4, axis=1)
    dx = ((k >> 3) - x + 4) & 3
    group = jnp.where(s == SLOTS, 3, jnp.where(dx == 0, 0, jnp.where(dx == 2, 2, 1)))
    key = ((group * 64 + jnp.where(live, cb, COL_BLOCKS)) * 128 + lanes) * 4 + rb
    across = jnp.broadcast_to(key, (BLOCK, BLOCK))
    down = across.T
    rank = jnp.sum((across < down).astype(jnp.int32), axis=1, keepdims=True)
    spot = lax.broadcasted_iota(jnp.int32, (BLOCK, BLOCK), 1)
    okey = jnp.sum(jnp.where(rank == spot, down, 0), axis=0, keepdims=True)
    oi = (okey >> 2) & 127
    ok, block = oi & 31, (okey >> 9) & 63
    odx, odz = ((ok >> 3) - x + 4) & 3, (((ok >> 1) & 3) - zh + 4) & 3
    before = pltpu.roll(block, 1, 1)
    first = (lanes == 0) | (lanes == GROUPS[1][0]) | (lanes == GROUPS[2][0])
    keep = jnp.where((block == before) & jnp.logical_not(first), 1, 0)
    zpos = jnp.where(odz == 0, 2, jnp.where(odz == 1, 0, jnp.where(odz == 2, 3, 1)))
    rows = [
        ok * SLOTS + (oi >> 5), jnp.where(odx == 3, 1, 0), (ok + h) & 1, zpos, okey & 3, keep,
    ]
    owner, column = down >> 15, (down >> 9) & 63
    wanted = (((spot >> 4) + zl) & 1) * 16 + (((spot >> 2) + y) & 3) * 4 + (spot & 3)
    for g, (begin, _) in enumerate(GROUPS):
        ours = owner == g
        upto = jnp.sum((ours & (column <= wanted)).astype(jnp.int32), axis=0, keepdims=True)
        here = jnp.sum((ours & (column == wanted)).astype(jnp.int32), axis=0, keepdims=True)
        rows.append(jnp.where(here > 0, begin + upto - 1, CELLS))
    return rows


def kernel(
    rowb, colb, counts, grad_hbm, feats_hbm, weight_hbm, adj_hbm, ig_out, wg_out,
    adj, halves, grad, feats, fhalves, weight, csum, wgt, wgl, wgf, ordered, meta,
    tiles, crossed, late0, late1, local_sem, send_sem, recv_sem, *bufs,
):
    n = len(CHUNKS)
    at = starts()
    chunk_bufs = [bufs[8 * j : 8 * (j + 1)] for j in range(n)]

    row, col = lax.axis_index("row"), lax.axis_index("col")
    x, zh, h = row // 8, (row // 2) % 4, row % 2
    zl, y = col // 4, col % 4
    deck = zh * 4 + zl * 2 + h
    pillar = x * 4 + y

    def chip(dx, dz):
        return {"row": ((x + dx) % 4) * 8 + ((zh + dz) % 4) * 2 + h, "col": col}

    def on_pillar(d):
        o = (pillar + d) % 16
        return {"row": (o // 4) * 8 + zh * 2 + h, "col": zl * 4 + o % 4}

    def on_deck(d):
        o = (deck + d) % 16
        return {"row": x * 8 + (o // 4) * 2 + o % 2, "col": ((o // 2) % 2) * 4 + y}

    def in_col(dzl, dy):
        return {"row": row, "col": ((zl + dzl) % 2) * 4 + (y + dy) % 4}

    sib = {"row": x * 8 + zh * 2 + 1 - h, "col": col}
    xp, xm, zp, zm = chip(1, 0), chip(3, 0), chip(0, 1), chip(0, 3)
    pillar_peers = [on_pillar(d) for d in range(1, 16)]
    deck_peers = [on_deck(d) for d in range(1, 16)]
    col_steps = [(a, b) for a in range(2) for b in range(4) if (a, b) != (0, 0)]
    col_peers = {step: in_col(*step) for step in col_steps}

    def load(k, src, dst):
        c = pltpu.make_async_copy(src, dst, local_sem.at[k])
        c.start()
        return c

    grad_load = load(0, grad_hbm, grad)
    adj_load = load(1, adj_hbm, adj)
    feats_load = load(2, feats_hbm, feats.at[0, 0])
    weight_load = load(3, weight_hbm, weight)

    barrier = pltpu.get_barrier_semaphore()
    greeted = pillar_peers + deck_peers + [col_peers[1, d] for d in range(1, 4)]
    for peer in greeted:
        pl.semaphore_signal(barrier, inc=1, device_id=peer, device_id_type=MESH)

    grad_load.wait()
    for rb in range(4):
        turned = grad[rb * BLOCK : (rb + 1) * BLOCK, :].T
        for j in range(n):
            chunk_bufs[j][0][0, 0, 2, rb] = turned[at[j] : at[j] + CHUNKS[j], :]
    pl.semaphore_wait(barrier, len(greeted))

    sends = []
    pending = {}

    def push(key, src, dst, peer):
        k = len(sends)
        c = pltpu.make_async_remote_copy(
            src_ref=src, dst_ref=dst, send_sem=send_sem.at[k], recv_sem=recv_sem.at[k],
            device_id=peer, device_id_type=MESH,
        )
        c.start()
        sends.append(c)
        pending.setdefault(key, []).append(c)

    def take(*key):
        for c in pending.pop(key):
            c.wait_recv()

    def stage_U(j, d):
        near, mid, far = chunk_bufs[j][:3]
        f, cross = CHUNKS[j], ACROSS[j]
        down, over = pl.ds(0, 4 - cross), pl.ds(4 - cross, cross)
        every = pl.ds(0, 4)

        def half(blocks, i):
            if cross:
                return blocks, pl.ds(i * (f // 2), f // 2)
            return (pl.ds(2 * i, 2),)

        def go(key, src, dst, peer, *index):
            push((key, j), src.at[index], dst.at[index], peer)

        own, plus, minus, both, opposite = 2, 0, 1, pl.ds(0, 2), 3
        if d == 0:
            unit = near.at[0, 0, own]
            go("X0", unit, mid.at[1, 0, own], xp, every)
            go("X0", unit, mid.at[0, 0, own], xm, every)
            go("Z0", unit, near.at[0, 0, minus], zp, every)
            go("Z0", unit, near.at[0, 0, plus], zm, every)
        elif d == 1:
            take("X0", j)
            go("1", mid.at[1, 0, own], far.at[0, 0, own], xp, *half(every, 0))
            go("1", mid.at[0, 0, own], far.at[0, 0, own], xm, *half(every, 1))
            if cross:
                pair = mid.at[:, 0, own, over]
                push(("1", j), pair, mid.at[:, 0, minus, over], zp)
                push(("1", j), pair, mid.at[:, 0, plus, over], zm)
            take("Z0", j)
            go("1", near.at[0, 0, minus], near.at[0, 0, opposite], zp, *half(every, 0))
            go("1", near.at[0, 0, plus], near.at[0, 0, opposite], zm, *half(every, 1))
            pair = near.at[0, 0, both, down]
            push(("1", j), pair, mid.at[1, 0, both, down], xp)
            push(("1", j), pair, mid.at[0, 0, both, down], xm)
        elif d == 2:
            take("1", j)
            push(("2", j), near.at[0, 0, opposite, down], mid.at[1, 0, opposite, down], xp)
            push(("2", j), near.at[0, 0, opposite, down], mid.at[0, 0, opposite, down], xm)
            go("2", mid.at[1, 0], far.at[0, 0], xp, both, *half(down, 0))
            go("2", mid.at[0, 0], far.at[0, 0], xm, both, *half(down, 1))
            if cross:
                push(("2", j), far.at[0, 0, own, over], far.at[0, 0, minus, over], zp)
                push(("2", j), far.at[0, 0, own, over], far.at[0, 0, plus, over], zm)
                lo, hi = half(over, 0), half(over, 1)
                push(("2", j), mid.at[:, 0, minus, *lo], mid.at[:, 0, opposite, *lo], zp)
                push(("2", j), mid.at[:, 0, plus, *hi], mid.at[:, 0, opposite, *hi], zm)
            push(("S", j, 0), near.at[:, 0], near.at[:, 1], sib)
        elif d == 3:
            take("2", j)
            go("3", mid.at[1, 0, opposite], far.at[0, 0, opposite], xp, *half(down, 0))
            go("3", mid.at[0, 0, opposite], far.at[0, 0, opposite], xm, *half(down, 1))
            if cross:
                go("3", far.at[0, 0, minus], far.at[0, 0, opposite], zp, *half(over, 0))
                go("3", far.at[0, 0, plus], far.at[0, 0, opposite], zm, *half(over, 1))
            push(("S", j, 1), mid.at[:, 0], mid.at[:, 1], sib)
        else:
            take("3", j)
            push(("S", j, 2), far.at[:, 0], far.at[:, 1], sib)

    def stage_C(j, part):
        group, begin, size = PARTS[part]
        g, run, f = chunk_bufs[j][group], chunk_bufs[j][7], CHUNKS[j]
        if begin == GROUPS[group][0]:
            take("S", j, group)
            init = jnp.zeros((f, BLOCK), jnp.float32)
        else:
            init = run[begin - 1]

        def step(p, acc):
            block = halves[meta[0, p]]
            high, low = split(g[meta[1, p] if group == 1 else 0, meta[2, p], meta[3, p], meta[4, p]])
            both = jnp.concatenate([high, low], axis=0).astype(jnp.bfloat16)
            r = jnp.dot(both, block, preferred_element_type=jnp.float32)
            product = r[:f, :BLOCK] + (r[f:, :BLOCK] + r[:f, BLOCK:])
            acc = product + jnp.where(meta[5, p] > 0, acc, 0.0)
            run[p] = acc
            return acc

        lax.fori_loop(begin, begin + size, step, init, unroll=24)

    def collect(j):
        part_sums, run = chunk_bufs[j][3], chunk_bufs[j][7]
        run[CELLS] = jnp.zeros((CHUNKS[j], BLOCK), jnp.float32)

        def body(m, carry):
            v = [run[meta[6 + g, m]] for g in range(3)]
            part_sums[m // 16, (m // 4) % 4, m % 4] = (v[0] + v[1]) + v[2]
            return carry

        lax.fori_loop(0, COL_BLOCKS, body, 0, unroll=8)

    def stage_R0(j):
        collect(j)
        p, landing, s, second = chunk_bufs[j][3:7]
        if ROUTES[j] == "direct":
            for i, (a, b) in enumerate(col_steps):
                push(("R0", j), p.at[a, b], landing.at[i], col_peers[a, b])
        elif ROUTES[j] == "z":
            push(("R0", j), p.at[1], second, col_peers[1, 0])
        else:
            for d in range(1, 4):
                push(("R0", j), p.at[:, d], landing.at[d - 1], col_peers[0, d])

    def stage_R1(j):
        p, landing, s, second = chunk_bufs[j][3:7]
        take("R0", j)
        if ROUTES[j] == "z":
            for d in (1, 2, 3, 0):
                s[d] = p[0, d] + second[d]
                if d:
                    push(("R1", j), s.at[d], landing.at[d - 1], col_peers[0, d])
        else:
            for z in (1, 0):
                s[z] = (p[z, 0] + landing[0, z]) + (landing[1, z] + landing[2, z])
                if z:
                    push(("R1", j), s.at[1], second, col_peers[1, 0])

    def stage_R2(j):
        p, landing, s, second = chunk_bufs[j][3:7]
        take("R0" if ROUTES[j] == "direct" else "R1", j)
        for b in range(4):
            if ROUTES[j] == "direct":
                v = p[0, 0, b]
                for i in range(7):
                    v += landing[i, b]
            elif ROUTES[j] == "z":
                v = (s[0, b] + landing[0, b]) + (landing[1, b] + landing[2, b])
            else:
                v = s[0, b] + second[b]
            csum[b, at[j] : at[j] + CHUNKS[j], :] = v

    def stage_F(i):
        first, rest = pl.ds(0, 2), pl.ds(2, 2)
        if i == 0:
            feats_load.wait()
            own = feats.at[0, 0]
            push(("F0",), own, feats.at[0, 3], col_peers[0, 1])
            push(("F0",), own, feats.at[0, 1], col_peers[0, 3])
            push(("Fz",), own, feats.at[1, 0], col_peers[1, 0])
        elif i == 1:
            take("Fz")
            push(("F1",), feats.at[1, 0], feats.at[1, 3], col_peers[0, 1])
            push(("F1",), feats.at[1, 0], feats.at[1, 1], col_peers[0, 3])
        elif i == 2:
            take("F0")
            push(("F2",), feats.at[0, 3, first], feats.at[0, 2, first], col_peers[0, 1])
            push(("F2",), feats.at[0, 1, rest], feats.at[0, 2, rest], col_peers[0, 3])
        elif i == 3:
            take("F1")
            push(("F3",), feats.at[1, 3, first], feats.at[1, 2, first], col_peers[0, 1])
            push(("F3",), feats.at[1, 1, rest], feats.at[1, 2, rest], col_peers[0, 3])
        else:
            take("F2")
            take("F3")

            def body(m, carry):
                high, low = split(feats[m // 16, (m // 4) % 4, m % 4])
                fhalves[m, :, :BLOCK] = high.astype(jnp.bfloat16)
                fhalves[m, :, BLOCK:] = low.astype(jnp.bfloat16)
                return carry

            lax.fori_loop(0, COL_BLOCKS, body, 0, unroll=2)

    def stage_G(j):
        f, p = CHUNKS[j], chunk_bufs[j][3]

        def body(m, total):
            high, low = split(p[m // 16, (m // 4) % 4, m % 4])
            both = jnp.concatenate([high, low], axis=0).astype(jnp.bfloat16)
            return total + jnp.dot(both, fhalves[m], preferred_element_type=jnp.float32)

        r = lax.fori_loop(
            0, COL_BLOCKS, body, jnp.zeros((2 * f, 2 * BLOCK), jnp.float32), unroll=8
        )
        total = r[:f, :BLOCK] + (r[f:, :BLOCK] + r[:f, BLOCK:])
        if j < EARLY:
            wgt[at[j] : at[j] + f, :] = total
        else:
            wgl[at[j] - at[EARLY] : at[j] - at[EARLY] + f, :] = total

    def fold(buf):
        total = buf[0]
        for i in range(1, 16):
            total += buf[i]
        return total

    def tile(ref, i):
        return ref.at[pl.ds(pl.multiple_of(i * 8, 8), 8)]

    def stage_V(i):
        if i == 0:
            wgt[at[EARLY] :, :] = jnp.zeros((WIDTH - at[EARLY], WIDTH), jnp.float32)
            for d in range(1, 16):
                to = (deck + d) % 16
                push(("V0",), tile(wgt, to), tiles.at[deck], deck_peers[d - 1])
            tiles[deck] = wgt[pl.ds(pl.multiple_of(deck * 8, 8), 8), :]
        elif i == 1:
            take("V0")
            crossed[pillar] = fold(tiles)
            for d in range(1, 16):
                push(("V1",), crossed.at[pillar], crossed.at[pillar], pillar_peers[d - 1])
        elif i == 2:
            take("V1")
            wgf[pl.ds(pl.multiple_of(deck * 8, 8), 8), :] = fold(crossed)
            for d in range(1, 16):
                push(("V2",), tile(wgf, deck), tile(wgf, deck), deck_peers[d - 1])
        else:
            take("V2")

    def stage_W(i):
        if i == 0:
            late0[deck] = wgl[...]
            for d in range(1, 16):
                push(("W0",), late0.at[deck], late0.at[deck], deck_peers[d - 1])
        elif i == 1:
            take("W0")
            late1[pillar] = fold(late0)
            for d in range(1, 16):
                push(("W1",), late1.at[pillar], late1.at[pillar], pillar_peers[d - 1])
        else:
            take("W1")

    parts, state = 8, {"done": 0, "sent": 0}

    def prepare():
        i = state["done"]
        state["done"] += 1
        if i == 0:
            ordered[...] = jnp.zeros((16, BLOCK), jnp.int32)
            for r, v in enumerate(order_slots(rowb, colb, counts, x, zh, h, zl, y)):
                ordered[r : r + 1, :] = v
            state["meta"] = load(4, ordered, meta)
            return
        if i == 1:
            adj_load.wait()
            state["meta"].wait()
        if i <= parts:
            size = CELLS // parts

            def body(s, carry):
                high, low = split(adj[s])
                halves[s, :, :BLOCK] = high.astype(jnp.bfloat16)
                halves[s, :, BLOCK:] = low.astype(jnp.bfloat16)
                return carry

            lax.fori_loop((i - 1) * size, i * size, body, 0, unroll=4)

    def drain(upto):
        while state["sent"] < upto:
            sends[state["sent"]].wait_send()
            state["sent"] += 1

    for name, j in ORDER:
        kind, i = name[0], int(name[1])
        if kind == "C":
            while state["done"] <= parts:
                prepare()
        if kind == "U":
            stage_U(j, i)
            prepare()
        elif kind == "C":
            stage_C(j, i)
        elif kind == "R":
            (stage_R0, stage_R1, stage_R2)[i](j)
        elif kind == "W":
            stage_W(i)
        elif kind == "F":
            stage_F(i)
        elif kind == "G":
            stage_G(j)
        elif kind == "V":
            stage_V(i)
            drain(len(sends) - 60)
        else:
            weight_load.wait()
            turned_weight = weight[...].T
            for b in range(4):
                ig_out[b * BLOCK : (b + 1) * BLOCK, :] = jnp.dot(
                    csum[b].T, turned_weight, precision=HIGHEST,
                    preferred_element_type=jnp.float32,
                )

    wg_out[...] = jnp.concatenate([wgf[: at[EARLY], :], fold(late1)], axis=0).T
    drain(len(sends))


def scratch():
    f32 = jnp.float32
    late = sum(CHUNKS[EARLY:])
    out = [
        pltpu.VMEM((CELLS, BLOCK, BLOCK), f32),
        pltpu.VMEM((CELLS, BLOCK, 2 * BLOCK), jnp.bfloat16),
        pltpu.VMEM((NODE_DEV, WIDTH), f32),
        pltpu.VMEM((2, 4, 4, BLOCK, WIDTH), f32),
        pltpu.VMEM((COL_BLOCKS, BLOCK, 2 * WIDTH), jnp.bfloat16),
        pltpu.VMEM((WIDTH, WIDTH), f32),
        pltpu.VMEM((4, WIDTH, BLOCK), f32),
        pltpu.VMEM((WIDTH, WIDTH), f32),
        pltpu.VMEM((late, WIDTH), f32),
        pltpu.VMEM((WIDTH, WIDTH), f32),
        pltpu.VMEM((16, BLOCK), jnp.int32),
        pltpu.SMEM((16, BLOCK), jnp.int32),
        pltpu.VMEM((16, 8, WIDTH), f32),
        pltpu.VMEM((16, 8, WIDTH), f32),
        pltpu.VMEM((16, late, WIDTH), f32),
        pltpu.VMEM((16, late, WIDTH), f32),
        pltpu.SemaphoreType.DMA((5,)),
    ]
    count = 34 * len(CHUNKS) + 90
    out += [pltpu.SemaphoreType.DMA((count,)), pltpu.SemaphoreType.DMA((count,))]
    for j, f in enumerate(CHUNKS):
        landing, summed, second = {
            "direct": ((7, 4), (1,), (1,)),
            "z": ((3, 4), (4, 4), (4, 4)),
            "y": ((3, 2, 4), (2, 4), (4,)),
        }[ROUTES[j]]
        for lead in (
            (1, 2, 4, 4), (2, 2, 4, 4), (1, 2, 4, 4), (2, 4, 4), landing, summed, second,
            (CELLS + 1,),
        ):
            out.append(pltpu.VMEM(lead + (f, BLOCK), f32))
    return out


def local(grad_out, features, weight, adj_values, row_block, col_block, counts):
    hbm = pl.BlockSpec(memory_space=pltpu.HBM)
    vmem = pl.BlockSpec(memory_space=pltpu.VMEM)
    return pl.pallas_call(
        kernel,
        out_shape=(
            jax.ShapeDtypeStruct((NODE_DEV, WIDTH), jnp.float32),
            jax.ShapeDtypeStruct((WIDTH, WIDTH), jnp.float32),
        ),
        in_specs=[vmem] * 3 + [hbm] * 4,
        out_specs=(vmem, vmem),
        scratch_shapes=scratch(),
        compiler_params=pltpu.CompilerParams(
            collective_id=0, has_side_effects=True, vmem_limit_bytes=60 * 1024 * 1024
        ),
        cost_estimate=pl.CostEstimate(
            flops=1_200_000_000, bytes_accessed=7_000_000, transcendentals=0
        ),
    )(
        row_block.transpose(2, 0, 1), col_block.transpose(2, 0, 1), counts, grad_out,
        features.reshape(4, BLOCK, WIDTH), weight,
        adj_values.reshape(CELLS, BLOCK, BLOCK),
    )


def solution(mesh):
    return jax.shard_map(
        local,
        mesh=mesh,
        in_specs=(
            P(("col", "row"), None),
            P(("row", "col"), None),
            P(),
            P("col", "row", None, None, None),
            P("col", "row", None),
            P("col", "row", None),
            P("col", "row"),
        ),
        out_specs=(P(("row", "col"), None), P()),
        check_vma=False,
    )
```

```python
import jax
import jax.numpy as jnp
from jax import lax
from jax.experimental import pallas as pl
from jax.experimental.pallas import tpu as pltpu
from jax.sharding import PartitionSpec as P

WIDTH = 128
BLOCK = 128
SLOTS = 3
SECTIONS = 32
CELLS = SECTIONS * SLOTS
GROUPS = ((0, 24), (24, 48), (72, 24))
PARTS = ((0, 0, 24), (1, 24, 24), (1, 48, 24), (2, 72, 24))
COL_BLOCKS = 32
NODE_DEV = 512
CHUNKS = (24, 40, 40, 24)
ACROSS = (0, 0, 1, 1)
ROUTES = ('y', 'y', 'y', 'z')
EARLY = 3
ORDER = (
    ("U0", 0), ("U0", 1), ("F0", 0), ("U1", 0), ("U1", 1), ("F1", 0), ("F2", 0), ("U0", 2), ("U2", 0), ("U0",
    3), ("C0", 0), ("U2", 1), ("C0", 1), ("F3", 0), ("U3", 0), ("U1", 2), ("C1", 0), ("C2", 0), ("U1", 3),
    ("U3", 1), ("U4", 0), ("F4", 0), ("C1", 1), ("C3", 0), ("R0", 0), ("U2", 2), ("G0", 0), ("C2", 1), ("C0",
    2), ("U2", 3), ("U4", 1), ("C0", 3), ("C3", 1), ("R0", 1), ("U3", 2), ("G0", 1), ("R1", 0), ("U3", 3),
    ("C1", 2), ("C2", 2), ("U4", 2), ("C1", 3), ("C2", 3), ("R2", 0), ("C3", 2), ("U4", 3), ("R0", 2), ("G0",
    2), ("V0", 0), ("C3", 3), ("R0", 3), ("G0", 3), ("W0", 0), ("R1", 1), ("V1", 0), ("R1", 3), ("R1", 2),
    ("R2", 1), ("W1", 0), ("V2", 0), ("R2", 3), ("R2", 2), ("O0", 0), ("W2", 0), ("V3", 0),
)
MESH = pl.DeviceIdType.MESH
HIGHEST = lax.Precision.HIGHEST


def starts():
    total, at = 0, []
    for f in CHUNKS:
        at.append(total)
        total += f
    return at


def split(v):
    high = v.astype(jnp.bfloat16).astype(jnp.float32)
    return high, v - high


def order_slots(rowb, colb, counts, x, zh, h, zl, y):
    lanes = lax.broadcasted_iota(jnp.int32, (1, BLOCK), 1)
    k, s = lanes & 31, lanes >> 5
    spare = jnp.zeros((1, SECTIONS), jnp.int32)

    def flat(ref):
        return jnp.concatenate([ref[0], ref[1], ref[2], spare], axis=1)

    rb, cb = flat(rowb), flat(colb)
    live = s < jnp.concatenate([counts[0:1, :]] * 4, axis=1)
    dx = ((k >> 3) - x + 4) & 3
    group = jnp.where(s == SLOTS, 3, jnp.where(dx == 0, 0, jnp.where(dx == 2, 2, 1)))
    key = ((group * 64 + jnp.where(live, cb, COL_BLOCKS)) * 128 + lanes) * 4 + rb
    across = jnp.broadcast_to(key, (BLOCK, BLOCK))
    down = across.T
    rank = jnp.sum((across < down).astype(jnp.int32), axis=1, keepdims=True)
    spot = lax.broadcasted_iota(jnp.int32, (BLOCK, BLOCK), 1)
    okey = jnp.sum(jnp.where(rank == spot, down, 0), axis=0, keepdims=True)
    oi = (okey >> 2) & 127
    ok, block = oi & 31, (okey >> 9) & 63
    odx, odz = ((ok >> 3) - x + 4) & 3, (((ok >> 1) & 3) - zh + 4) & 3
    before = pltpu.roll(block, 1, 1)
    first = (lanes == 0) | (lanes == GROUPS[1][0]) | (lanes == GROUPS[2][0])
    keep = jnp.where((block == before) & jnp.logical_not(first), 1, 0)
    zpos = jnp.where(odz == 0, 2, jnp.where(odz == 1, 0, jnp.where(odz == 2, 3, 1)))
    rows = [
        ok * SLOTS + (oi >> 5), jnp.where(odx == 3, 1, 0), (ok + h) & 1, zpos, okey & 3, keep,
    ]
    owner, column = down >> 15, (down >> 9) & 63
    wanted = (((spot >> 4) + zl) & 1) * 16 + (((spot >> 2) + y) & 3) * 4 + (spot & 3)
    for g, (begin, _) in enumerate(GROUPS):
        ours = owner == g
        upto = jnp.sum((ours & (column <= wanted)).astype(jnp.int32), axis=0, keepdims=True)
        here = jnp.sum((ours & (column == wanted)).astype(jnp.int32), axis=0, keepdims=True)
        rows.append(jnp.where(here > 0, begin + upto - 1, CELLS))
    return rows


def kernel(
    rowb, colb, counts, grad_hbm, feats_hbm, weight_hbm, adj_hbm, ig_out, wg_out,
    adj, halves, grad, feats, fhalves, weight, csum, ig, wgt, wgl, wgf, ordered, meta,
    tiles, crossed, late0, late1, local_sem, send_sem, recv_sem, *bufs,
):
    n = len(CHUNKS)
    at = starts()
    chunk_bufs = [bufs[8 * j : 8 * (j + 1)] for j in range(n)]

    row, col = lax.axis_index("row"), lax.axis_index("col")
    x, zh, h = row // 8, (row // 2) % 4, row % 2
    zl, y = col // 4, col % 4
    deck = zh * 4 + zl * 2 + h
    pillar = x * 4 + y

    def chip(dx, dz):
        return {"row": ((x + dx) % 4) * 8 + ((zh + dz) % 4) * 2 + h, "col": col}

    def on_pillar(d):
        o = (pillar + d) % 16
        return {"row": (o // 4) * 8 + zh * 2 + h, "col": zl * 4 + o % 4}

    def on_deck(d):
        o = (deck + d) % 16
        return {"row": x * 8 + (o // 4) * 2 + o % 2, "col": ((o // 2) % 2) * 4 + y}

    def in_col(dzl, dy):
        return {"row": row, "col": ((zl + dzl) % 2) * 4 + (y + dy) % 4}

    sib = {"row": x * 8 + zh * 2 + 1 - h, "col": col}
    xp, xm, zp, zm = chip(1, 0), chip(3, 0), chip(0, 1), chip(0, 3)
    pillar_peers = [on_pillar(d) for d in range(1, 16)]
    deck_peers = [on_deck(d) for d in range(1, 16)]
    col_steps = [(a, b) for a in range(2) for b in range(4) if (a, b) != (0, 0)]
    col_peers = {step: in_col(*step) for step in col_steps}

    def load(k, src, dst):
        c = pltpu.make_async_copy(src, dst, local_sem.at[k])
        c.start()
        return c

    grad_load = load(0, grad_hbm, grad)
    adj_load = load(1, adj_hbm, adj)
    feats_load = load(2, feats_hbm, feats.at[0, 0])
    weight_load = load(3, weight_hbm, weight)

    barrier = pltpu.get_barrier_semaphore()
    greeted = pillar_peers + deck_peers + [col_peers[1, d] for d in range(1, 4)]
    for peer in greeted:
        pl.semaphore_signal(barrier, inc=1, device_id=peer, device_id_type=MESH)

    grad_load.wait()
    for rb in range(4):
        turned = grad[rb * BLOCK : (rb + 1) * BLOCK, :].T
        for j in range(n):
            chunk_bufs[j][0][0, 0, 2, rb] = turned[at[j] : at[j] + CHUNKS[j], :]
    pl.semaphore_wait(barrier, len(greeted))

    sends = []
    pending = {}

    def push(key, src, dst, peer):
        k = len(sends)
        c = pltpu.make_async_remote_copy(
            src_ref=src, dst_ref=dst, send_sem=send_sem.at[k], recv_sem=recv_sem.at[k],
            device_id=peer, device_id_type=MESH,
        )
        c.start()
        sends.append(c)
        pending.setdefault(key, []).append(c)

    def take(*key):
        for c in pending.pop(key):
            c.wait_recv()

    def stage_U(j, d):
        near, mid, far = chunk_bufs[j][:3]
        f, cross = CHUNKS[j], ACROSS[j]
        down, over = pl.ds(0, 4 - cross), pl.ds(4 - cross, cross)
        every = pl.ds(0, 4)

        def half(blocks, i):
            if cross:
                return blocks, pl.ds(i * (f // 2), f // 2)
            return (pl.ds(2 * i, 2),)

        def go(key, src, dst, peer, *index):
            push((key, j), src.at[index], dst.at[index], peer)

        own, plus, minus, both, opposite = 2, 0, 1, pl.ds(0, 2), 3
        if d == 0:
            unit = near.at[0, 0, own]
            go("X0", unit, mid.at[1, 0, own], xp, every)
            go("X0", unit, mid.at[0, 0, own], xm, every)
            go("Z0", unit, near.at[0, 0, minus], zp, every)
            go("Z0", unit, near.at[0, 0, plus], zm, every)
        elif d == 1:
            take("X0", j)
            go("1", mid.at[1, 0, own], far.at[0, 0, own], xp, *half(every, 0))
            go("1", mid.at[0, 0, own], far.at[0, 0, own], xm, *half(every, 1))
            if cross:
                pair = mid.at[:, 0, own, over]
                push(("1", j), pair, mid.at[:, 0, minus, over], zp)
                push(("1", j), pair, mid.at[:, 0, plus, over], zm)
            take("Z0", j)
            go("1", near.at[0, 0, minus], near.at[0, 0, opposite], zp, *half(every, 0))
            go("1", near.at[0, 0, plus], near.at[0, 0, opposite], zm, *half(every, 1))
            pair = near.at[0, 0, both, down]
            push(("1", j), pair, mid.at[1, 0, both, down], xp)
            push(("1", j), pair, mid.at[0, 0, both, down], xm)
        elif d == 2:
            take("1", j)
            push(("2", j), near.at[0, 0, opposite, down], mid.at[1, 0, opposite, down], xp)
            push(("2", j), near.at[0, 0, opposite, down], mid.at[0, 0, opposite, down], xm)
            go("2", mid.at[1, 0], far.at[0, 0], xp, both, *half(down, 0))
            go("2", mid.at[0, 0], far.at[0, 0], xm, both, *half(down, 1))
            if cross:
                push(("2", j), far.at[0, 0, own, over], far.at[0, 0, minus, over], zp)
                push(("2", j), far.at[0, 0, own, over], far.at[0, 0, plus, over], zm)
                lo, hi = half(over, 0), half(over, 1)
                push(("2", j), mid.at[:, 0, minus, *lo], mid.at[:, 0, opposite, *lo], zp)
                push(("2", j), mid.at[:, 0, plus, *hi], mid.at[:, 0, opposite, *hi], zm)
            push(("S", j, 0), near.at[:, 0], near.at[:, 1], sib)
        elif d == 3:
            take("2", j)
            go("3", mid.at[1, 0, opposite], far.at[0, 0, opposite], xp, *half(down, 0))
            go("3", mid.at[0, 0, opposite], far.at[0, 0, opposite], xm, *half(down, 1))
            if cross:
                go("3", far.at[0, 0, minus], far.at[0, 0, opposite], zp, *half(over, 0))
                go("3", far.at[0, 0, plus], far.at[0, 0, opposite], zm, *half(over, 1))
            push(("S", j, 1), mid.at[:, 0], mid.at[:, 1], sib)
        else:
            take("3", j)
            push(("S", j, 2), far.at[:, 0], far.at[:, 1], sib)

    def stage_C(j, part):
        group, begin, size = PARTS[part]
        g, run, f = chunk_bufs[j][group], chunk_bufs[j][7], CHUNKS[j]
        if begin == GROUPS[group][0]:
            take("S", j, group)
            init = jnp.zeros((f, BLOCK), jnp.float32)
        else:
            init = run[begin - 1]

        def step(p, acc):
            block = halves[meta[0, p]]
            high, low = split(g[meta[1, p] if group == 1 else 0, meta[2, p], meta[3, p], meta[4, p]])
            both = jnp.concatenate([high, low], axis=0).astype(jnp.bfloat16)
            r = jnp.dot(both, block, preferred_element_type=jnp.float32)
            product = r[:f, :BLOCK] + (r[f:, :BLOCK] + r[:f, BLOCK:])
            acc = product + jnp.where(meta[5, p] > 0, acc, 0.0)
            run[p] = acc
            return acc

        lax.fori_loop(begin, begin + size, step, init, unroll=24)

    def collect(j):
        part_sums, run = chunk_bufs[j][3], chunk_bufs[j][7]
        run[CELLS] = jnp.zeros((CHUNKS[j], BLOCK), jnp.float32)

        def body(m, carry):
            v = [run[meta[6 + g, m]] for g in range(3)]
            part_sums[m // 16, (m // 4) % 4, m % 4] = (v[0] + v[1]) + v[2]
            return carry

        lax.fori_loop(0, COL_BLOCKS, body, 0, unroll=8)

    def stage_R0(j):
        collect(j)
        p, landing, s, second = chunk_bufs[j][3:7]
        if ROUTES[j] == "direct":
            for i, (a, b) in enumerate(col_steps):
                push(("R0", j), p.at[a, b], landing.at[i], col_peers[a, b])
        elif ROUTES[j] == "z":
            push(("R0", j), p.at[1], second, col_peers[1, 0])
        else:
            for d in range(1, 4):
                push(("R0", j), p.at[:, d], landing.at[d - 1], col_peers[0, d])

    def stage_R1(j):
        p, landing, s, second = chunk_bufs[j][3:7]
        take("R0", j)
        if ROUTES[j] == "z":
            for d in (1, 2, 3, 0):
                s[d] = p[0, d] + second[d]
                if d:
                    push(("R1", j), s.at[d], landing.at[d - 1], col_peers[0, d])
        else:
            for z in (1, 0):
                s[z] = (p[z, 0] + landing[0, z]) + (landing[1, z] + landing[2, z])
                if z:
                    push(("R1", j), s.at[1], second, col_peers[1, 0])

    def stage_R2(j):
        p, landing, s, second = chunk_bufs[j][3:7]
        take("R0" if ROUTES[j] == "direct" else "R1", j)
        for b in range(4):
            if ROUTES[j] == "direct":
                v = p[0, 0, b]
                for i in range(7):
                    v += landing[i, b]
            elif ROUTES[j] == "z":
                v = (s[0, b] + landing[0, b]) + (landing[1, b] + landing[2, b])
            else:
                v = s[0, b] + second[b]
            csum[b, at[j] : at[j] + CHUNKS[j], :] = v

    def stage_F(i):
        first, rest = pl.ds(0, 2), pl.ds(2, 2)
        if i == 0:
            feats_load.wait()
            own = feats.at[0, 0]
            push(("F0",), own, feats.at[0, 3], col_peers[0, 1])
            push(("F0",), own, feats.at[0, 1], col_peers[0, 3])
            push(("Fz",), own, feats.at[1, 0], col_peers[1, 0])
        elif i == 1:
            take("Fz")
            push(("F1",), feats.at[1, 0], feats.at[1, 3], col_peers[0, 1])
            push(("F1",), feats.at[1, 0], feats.at[1, 1], col_peers[0, 3])
        elif i == 2:
            take("F0")
            push(("F2",), feats.at[0, 3, first], feats.at[0, 2, first], col_peers[0, 1])
            push(("F2",), feats.at[0, 1, rest], feats.at[0, 2, rest], col_peers[0, 3])
        elif i == 3:
            take("F1")
            push(("F3",), feats.at[1, 3, first], feats.at[1, 2, first], col_peers[0, 1])
            push(("F3",), feats.at[1, 1, rest], feats.at[1, 2, rest], col_peers[0, 3])
        else:
            take("F2")
            take("F3")

            def body(m, carry):
                high, low = split(feats[m // 16, (m // 4) % 4, m % 4])
                fhalves[m, :, :BLOCK] = high.astype(jnp.bfloat16)
                fhalves[m, :, BLOCK:] = low.astype(jnp.bfloat16)
                return carry

            lax.fori_loop(0, COL_BLOCKS, body, 0, unroll=2)

    def stage_G(j):
        f, p = CHUNKS[j], chunk_bufs[j][3]

        def body(m, total):
            high, low = split(p[m // 16, (m // 4) % 4, m % 4])
            both = jnp.concatenate([high, low], axis=0).astype(jnp.bfloat16)
            return total + jnp.dot(both, fhalves[m], preferred_element_type=jnp.float32)

        r = lax.fori_loop(
            0, COL_BLOCKS, body, jnp.zeros((2 * f, 2 * BLOCK), jnp.float32), unroll=8
        )
        total = r[:f, :BLOCK] + (r[f:, :BLOCK] + r[:f, BLOCK:])
        if j < EARLY:
            wgt[at[j] : at[j] + f, :] = total
        else:
            wgl[at[j] - at[EARLY] : at[j] - at[EARLY] + f, :] = total

    def fold(buf):
        total = buf[0]
        for i in range(1, 16):
            total += buf[i]
        return total

    def tile(ref, i):
        return ref.at[pl.ds(pl.multiple_of(i * 8, 8), 8)]

    def stage_V(i):
        if i == 0:
            wgt[at[EARLY] :, :] = jnp.zeros((WIDTH - at[EARLY], WIDTH), jnp.float32)
            for d in range(1, 16):
                to = (deck + d) % 16
                push(("V0",), tile(wgt, to), tiles.at[deck], deck_peers[d - 1])
            tiles[deck] = wgt[pl.ds(pl.multiple_of(deck * 8, 8), 8), :]
        elif i == 1:
            take("V0")
            crossed[pillar] = fold(tiles)
            for d in range(1, 16):
                push(("V1",), crossed.at[pillar], crossed.at[pillar], pillar_peers[d - 1])
        elif i == 2:
            take("V1")
            wgf[pl.ds(pl.multiple_of(deck * 8, 8), 8), :] = fold(crossed)
            for d in range(1, 16):
                push(("V2",), tile(wgf, deck), tile(wgf, deck), deck_peers[d - 1])
        else:
            take("V2")

    def stage_W(i):
        if i == 0:
            late0[deck] = wgl[...]
            for d in range(1, 16):
                push(("W0",), late0.at[deck], late0.at[deck], deck_peers[d - 1])
        elif i == 1:
            take("W0")
            late1[pillar] = fold(late0)
            for d in range(1, 16):
                push(("W1",), late1.at[pillar], late1.at[pillar], pillar_peers[d - 1])
        else:
            take("W1")

    parts, state = 8, {"done": 0, "sent": 0}

    def prepare():
        i = state["done"]
        state["done"] += 1
        if i == 0:
            ordered[...] = jnp.zeros((16, BLOCK), jnp.int32)
            for r, v in enumerate(order_slots(rowb, colb, counts, x, zh, h, zl, y)):
                ordered[r : r + 1, :] = v
            state["meta"] = load(4, ordered, meta)
            return
        if i == 1:
            adj_load.wait()
            state["meta"].wait()
        if i <= parts:
            size = CELLS // parts

            def body(s, carry):
                high, low = split(adj[s])
                halves[s, :, :BLOCK] = high.astype(jnp.bfloat16)
                halves[s, :, BLOCK:] = low.astype(jnp.bfloat16)
                return carry

            lax.fori_loop((i - 1) * size, i * size, body, 0, unroll=4)

    def drain(upto):
        while state["sent"] < upto:
            sends[state["sent"]].wait_send()
            state["sent"] += 1

    for name, j in ORDER:
        kind, i = name[0], int(name[1])
        if kind == "C":
            while state["done"] <= parts:
                prepare()
        if kind == "U":
            stage_U(j, i)
            prepare()
        elif kind == "C":
            stage_C(j, i)
        elif kind == "R":
            (stage_R0, stage_R1, stage_R2)[i](j)
        elif kind == "W":
            stage_W(i)
        elif kind == "F":
            stage_F(i)
        elif kind == "G":
            stage_G(j)
        elif kind == "V":
            stage_V(i)
            if i:
                drain(len(sends) - 60 if i < 3 else len(sends) - 15)
        else:
            weight_load.wait()
            turned_weight = weight[...].T
            for b in range(4):
                ig[b * BLOCK : (b + 1) * BLOCK, :] = jnp.dot(
                    csum[b].T, turned_weight, precision=HIGHEST,
                    preferred_element_type=jnp.float32,
                )
            ig_store = load(0, ig, ig_out)

    wg_out[...] = jnp.concatenate([wgf[: at[EARLY], :], fold(late1)], axis=0).T
    drain(len(sends))
    ig_store.wait()


def scratch():
    f32 = jnp.float32
    late = sum(CHUNKS[EARLY:])
    out = [
        pltpu.VMEM((CELLS, BLOCK, BLOCK), f32),
        pltpu.VMEM((CELLS, BLOCK, 2 * BLOCK), jnp.bfloat16),
        pltpu.VMEM((NODE_DEV, WIDTH), f32),
        pltpu.VMEM((2, 4, 4, BLOCK, WIDTH), f32),
        pltpu.VMEM((COL_BLOCKS, BLOCK, 2 * WIDTH), jnp.bfloat16),
        pltpu.VMEM((WIDTH, WIDTH), f32),
        pltpu.VMEM((4, WIDTH, BLOCK), f32),
        pltpu.VMEM((NODE_DEV, WIDTH), f32),
        pltpu.VMEM((WIDTH, WIDTH), f32),
        pltpu.VMEM((late, WIDTH), f32),
        pltpu.VMEM((WIDTH, WIDTH), f32),
        pltpu.VMEM((16, BLOCK), jnp.int32),
        pltpu.SMEM((16, BLOCK), jnp.int32),
        pltpu.VMEM((16, 8, WIDTH), f32),
        pltpu.VMEM((16, 8, WIDTH), f32),
        pltpu.VMEM((16, late, WIDTH), f32),
        pltpu.VMEM((16, late, WIDTH), f32),
        pltpu.SemaphoreType.DMA((5,)),
    ]
    count = 34 * len(CHUNKS) + 90
    out += [pltpu.SemaphoreType.DMA((count,)), pltpu.SemaphoreType.DMA((count,))]
    for j, f in enumerate(CHUNKS):
        landing, summed, second = {
            "direct": ((7, 4), (1,), (1,)),
            "z": ((3, 4), (4, 4), (4, 4)),
            "y": ((3, 2, 4), (2, 4), (4,)),
        }[ROUTES[j]]
        for lead in (
            (1, 2, 4, 4), (2, 2, 4, 4), (1, 2, 4, 4), (2, 4, 4), landing, summed, second,
            (CELLS + 1,),
        ):
            out.append(pltpu.VMEM(lead + (f, BLOCK), f32))
    return out


def local(grad_out, features, weight, adj_values, row_block, col_block, counts):
    hbm = pl.BlockSpec(memory_space=pltpu.HBM)
    vmem = pl.BlockSpec(memory_space=pltpu.VMEM)
    return pl.pallas_call(
        kernel,
        out_shape=(
            jax.ShapeDtypeStruct((NODE_DEV, WIDTH), jnp.float32),
            jax.ShapeDtypeStruct((WIDTH, WIDTH), jnp.float32),
        ),
        in_specs=[vmem] * 3 + [hbm] * 4,
        out_specs=(pl.BlockSpec(memory_space=pl.ANY), vmem),
        scratch_shapes=scratch(),
        compiler_params=pltpu.CompilerParams(
            collective_id=0, has_side_effects=True, vmem_limit_bytes=60 * 1024 * 1024
        ),
        cost_estimate=pl.CostEstimate(
            flops=1_200_000_000, bytes_accessed=7_000_000, transcendentals=0
        ),
    )(
        row_block.transpose(2, 0, 1), col_block.transpose(2, 0, 1), counts, grad_out,
        features.reshape(4, BLOCK, WIDTH), weight,
        adj_values.reshape(CELLS, BLOCK, BLOCK),
    )


def solution(mesh):
    return jax.shard_map(
        local,
        mesh=mesh,
        in_specs=(
            P(("col", "row"), None),
            P(("row", "col"), None),
            P(),
            P("col", "row", None, None, None),
            P("col", "row", None),
            P("col", "row", None),
            P("col", "row"),
        ),
        out_specs=(P(("row", "col"), None), P()),
        check_vma=False,
    )
```
